32 devices in a mesh: groups: 2 (over x), row: 4 (over z), col: 4 (over y, core).
Axes of the slice: x: 2, y: 2, z: 4, core: 2. Of those that a mesh axis runs over, the one named last changes fastest.
Arguments:
- pair: bfloat16 [288, 144, 128], P(('groups', 'row'), 'col'), parts along dimension 0, may hold values from -6 to 6
- token_mask: int32 [288], P('groups'), parts along dimension 0, may hold values 0 or 1
- in_gain: float32 [128], replicated, may hold values from 0.1 to 1.9
- in_bias: float32 [128], replicated, may hold values from -3 to 3
- w_in: bfloat16 [128, 512], replicated, may hold values from -0.5 to 0.5
- w_gate: bfloat16 [128, 128], replicated, may hold values from -0.5 to 0.5
- out_gain: float32 [128], replicated, may hold values from 0.1 to 1.9
- out_bias: float32 [128], replicated, may hold values from -3 to 3
- w_out: bfloat16 [128, 128], replicated, may hold values from -0.5 to 0.5
Outputs:
- update: bfloat16 [288, 144, 128], P(('groups', 'row'), 'col'), parts along dimension 0
The draws below stay inside these ranges and needn't reach their ends.
There are 2 independent parts, one for each index of `groups`. The reference program is written for one: setup_inputs(seed, part) draws one part's arguments, and reference() takes and returns one part's arrays. A program takes and returns all parts, laid end to end along the dimension named above; an argument that names none is the same for every part. Nothing has to cross between parts.
Inputs may be any that keep to these rules, and one draw needn't show every extreme that they name: `token_mask`: one 0/1 residue flag per token.
All inputs are finite; a program needn't handle non-finite values.
Results may differ from the reference program's by a relative error of at most 0.0052.
Values may be sent and summed in bfloat16 or wider, within the bound.
A program may use at most 128 MiB of HBM per device.

```python
import jax
import jax.numpy as jnp
from jax import lax

PAIR_DIM = 128
HIDDEN_SIZE = 128
TOKENS = 144


def touch_ends(result, key, low, high):
    dims = result.shape
    index_at = [jax.random.randint(jax.random.fold_in(key, axis), (), 0, dims[axis]) for axis in range(len(dims))]
    result = result.at[tuple(index_at)].set(low)
    longest = dims.index(max(dims))
    index_at[longest] = (index_at[longest] + 1) % dims[longest]
    return result.at[tuple(index_at)].set(high)


def steps_of(own_key, dims, shards, low, largest):
    loudness = 1.0
    for axis_at, parts in shards:
        heights = jax.random.uniform(jax.random.fold_in(jax.random.fold_in(own_key, 6), axis_at), (parts,), jnp.float32, low / len(shards), largest / len(shards))
        loudness = loudness * jnp.repeat(jnp.exp(heights), dims[axis_at] // parts).reshape((-1,) + (1,) * (len(dims) - 1 - axis_at))
    return loudness


def bell_draw(key, extent, scale, limit, pieces=(), held_as=jnp.bfloat16):
    level = steps_of(key, extent, pieces, -0.22, 0.18) if pieces else 1.0
    values = jax.random.normal(key, extent, jnp.float32) * scale * level
    return jnp.minimum(jnp.maximum(values, -limit), limit).astype(held_as)


def setup_inputs(seed: int = 0, part: int = 0) -> dict:
    seeds = jax.random.split(jax.random.key(seed), 10)
    part_splits = jax.random.split(jax.random.fold_in(seeds[9], part), 10)
    return {
        "pair": bell_draw(part_splits[0], (TOKENS, TOKENS, PAIR_DIM), 1.0, 6.0, ((0, 4), (1, 4))),
        "token_mask": touch_ends((jax.random.randint(part_splits[1], (TOKENS,), 0, 4) < 3).astype(jnp.int32), jax.random.fold_in(part_splits[1], 1), 0, 1),
        "in_gain": jnp.clip(1.0 + 0.18 * jax.random.normal(seeds[2], (PAIR_DIM,), jnp.float32), 0.1, 1.9),
        "in_bias": bell_draw(seeds[3], (PAIR_DIM,), 0.5, 3.0, (), jnp.float32),
        "w_in": bell_draw(seeds[4], (PAIR_DIM, 4 * HIDDEN_SIZE), PAIR_DIM ** -0.5, 0.5),
        "w_gate": bell_draw(seeds[5], (PAIR_DIM, PAIR_DIM), PAIR_DIM ** -0.5, 0.5),
        "out_gain": jnp.clip(1.0 + 0.18 * jax.random.normal(seeds[6], (HIDDEN_SIZE,), jnp.float32), 0.1, 1.9),
        "out_bias": bell_draw(seeds[7], (HIDDEN_SIZE,), 0.5, 3.0, (), jnp.float32),
        "w_out": bell_draw(seeds[8], (HIDDEN_SIZE, PAIR_DIM), HIDDEN_SIZE ** -0.5, 0.5),
    }


def layer_norm(values, gain, bias):
    average = lax.optimization_barrier(jnp.mean(values, axis=-1, keepdims=True))
    centred = values - average
    variance = lax.optimization_barrier(jnp.mean(centred * centred, axis=-1, keepdims=True))
    return centred * lax.rsqrt(variance + 1e-05) * gain + bias

def reference(pair, token_mask, in_gain, in_bias, w_in, w_gate, out_gain, out_bias, w_out):
    normed = layer_norm(pair.astype(jnp.float32), in_gain, in_bias).astype(jnp.bfloat16)
    flat = normed.reshape(TOKENS * TOKENS, PAIR_DIM)
    proj = jnp.dot(flat, w_in, preferred_element_type=jnp.float32).reshape(TOKENS, TOKENS, 4, HIDDEN_SIZE)
    flags = token_mask.astype(jnp.float32)
    pmask = (flags[:, None] * flags[None, :])[:, :, None]
    left = (jax.nn.sigmoid(proj[:, :, 0]) * proj[:, :, 1] * pmask).astype(jnp.bfloat16)
    right = (jax.nn.sigmoid(proj[:, :, 2]) * proj[:, :, 3] * pmask).astype(jnp.bfloat16)
    triangle = jnp.einsum('ikh,jkh->ijh', left.astype(jnp.float32), right.astype(jnp.float32))
    tnorm = layer_norm(triangle, out_gain, out_bias).astype(jnp.bfloat16)
    gating = jax.nn.sigmoid(jnp.dot(flat, w_gate, preferred_element_type=jnp.float32))
    projected = jnp.dot(tnorm.reshape(TOKENS * TOKENS, HIDDEN_SIZE), w_out, preferred_element_type=jnp.float32)
    return (gating * projected).reshape(TOKENS, TOKENS, PAIR_DIM).astype(jnp.bfloat16)
```

```python
import functools

import jax
import jax.numpy as jnp
from jax import lax
from jax.experimental import pallas as pl
from jax.experimental.pallas import tpu as pltpu
from jax.sharding import PartitionSpec as P

MESH = pl.DeviceIdType.MESH
JTILE = 4


def sigmoid(values):
    return 0.5 * jnp.tanh(0.5 * values) + 0.5


def layer_norm(values, gain, bias):
    average = jnp.mean(values, axis=-1, keepdims=True)
    centred = values - average
    variance = jnp.mean(centred * centred, axis=-1, keepdims=True)
    return centred * lax.rsqrt(variance + 1e-05) * gain + bias


def kernel(
    nrow, ncol, row_tok, col_tok, parts,
    pair_ref, pair_t_ref, mask_ref, mask_t_ref, in_gain, in_bias, w_in, w_gate, out_gain, out_bias, w_out,
    out_ref,
    blocks, left, gate, wide, stage, sums_out, sums_own, sums_in,
    z_send, z_recv, p_send, p_recv,
):
    hidden = w_out.shape[0]
    group, row, col = lax.axis_index("groups"), lax.axis_index("row"), lax.axis_index("col")
    per_row = row_tok // col_tok
    chunks = per_row * parts
    chunk_j = col_tok // parts
    rows = chunk_j * col_tok
    sum_rows = chunk_j * row_tok
    has_up, has_down = row < nrow - 1, row > 0

    barrier = pltpu.get_barrier_semaphore()

    @pl.when(has_up)
    def _():
        pl.semaphore_signal(barrier, inc=1, device_id=(group, row + 1, col), device_id_type=MESH)

    @pl.when(has_down)
    def _():
        pl.semaphore_signal(barrier, inc=1, device_id=(group, row - 1, col), device_id_type=MESH)

    for step in range(1, ncol):
        peer = lax.rem(col + step, ncol)
        pl.semaphore_signal(barrier, inc=1, device_id=(group, row, peer), device_id_type=MESH)

    def up_copy(block, chunk):
        at = blocks.at[block, chunk]
        return pltpu.make_async_remote_copy(
            at, at, z_send.at[0, block, chunk], z_recv.at[block, chunk], (group, row + 1, col), MESH
        )

    def down_copy(block, chunk):
        at = blocks.at[block, chunk]
        return pltpu.make_async_remote_copy(
            at, at, z_send.at[1, block, chunk], z_recv.at[block, chunk], (group, row - 1, col), MESH
        )

    def sum_copy(target, source, part):
        return pltpu.make_async_remote_copy(
            sums_out.at[target, part], sums_in.at[source, part],
            p_send.at[target, part], p_recv.at[source, part], (group, row, target), MESH,
        )

    gain, bias = in_gain[...], in_bias[...]

    for chunk in range(chunks):
        span = pl.ds(chunk * rows, rows)
        normed = layer_norm(pair_ref[span, :].astype(jnp.float32), gain, bias).astype(jnp.bfloat16)
        proj = jnp.dot(normed, w_in[:, 2 * hidden :], preferred_element_type=jnp.float32)
        right = sigmoid(proj[:, :hidden]) * proj[:, hidden:] * mask_ref[span, :]
        blocks[row, chunk] = right.astype(jnp.bfloat16)
        if chunk == 0:
            neighbours = has_up.astype(jnp.int32) + has_down.astype(jnp.int32)
            pl.semaphore_wait(barrier, ncol - 1 + neighbours)

        @pl.when(has_up)
        def _():
            up_copy(row, chunk).start()

        @pl.when(has_down)
        def _():
            down_copy(row, chunk).start()

    k_step = col_tok // parts
    for part in range(parts):
        span = pl.ds(part * sum_rows, sum_rows)
        normed = layer_norm(pair_t_ref[span, :].astype(jnp.float32), gain, bias).astype(jnp.bfloat16)
        proj = jnp.dot(normed, w_in[:, : 2 * hidden], preferred_element_type=jnp.float32)
        value = sigmoid(proj[:, :hidden]) * proj[:, hidden:] * mask_t_ref[span, :]
        value = value.astype(jnp.bfloat16).astype(jnp.float32)
        for k in range(k_step):
            left[part * k_step + k, :row_tok, :] = value[k * row_tok : (k + 1) * row_tok]
        gate[span, :] = sigmoid(jnp.dot(normed, w_gate[...], preferred_element_type=jnp.float32))

    def partial_sums(block, chunk):
        target, part = block * per_row + chunk // parts, lax.rem(chunk, parts)
        wide[...] = blocks[block, chunk].astype(jnp.float32)

        def tile(at, carry):
            start = pl.multiple_of(at * (JTILE * col_tok), 16)
            totals = [jnp.zeros((row_tok, hidden), jnp.float32) for _ in range(JTILE)]
            for k in range(col_tok):
                lines = left[k, :row_tok, :]
                for j in range(JTILE):
                    totals[j] += wide[pl.ds(start + (j * col_tok + k), 1), :] * lines
            for j in range(JTILE):
                stage[j * row_tok : (j + 1) * row_tok, :] = totals[j]
            span = pl.ds(pl.multiple_of(at * (JTILE * row_tok), 16), JTILE * row_tok)

            @pl.when(target == col)
            def _():
                sums_own[part, span, :] = stage[...]

            @pl.when(target != col)
            def _():
                sums_out[target, part, span, :] = stage[...].astype(jnp.bfloat16)

            return carry

        lax.fori_loop(0, chunk_j // JTILE, tile, 0)

        @pl.when(target != col)
        def _():
            sum_copy(target, col, part).start()

    def own_step(chunk, carry):
        partial_sums(row, chunk)
        return carry

    lax.fori_loop(0, chunks, own_step, 0)

    def arrival(index, carry):
        step = index // (2 * chunks) + 1
        within = lax.rem(index, 2 * chunks)
        chunk, above = within // 2, lax.rem(within, 2)
        block = row - step + above * (2 * step)

        @pl.when((block >= 0) & (block < nrow))
        def _():
            @pl.when(above == 0)
            def _():
                down_copy(block, chunk).wait_recv()

                @pl.when(has_up)
                def _():
                    up_copy(block, chunk).start()

            @pl.when(above == 1)
            def _():
                up_copy(block, chunk).wait_recv()

                @pl.when(has_down)
                def _():
                    down_copy(block, chunk).start()

            partial_sums(block, chunk)

        return carry

    lax.fori_loop(0, 2 * chunks * (nrow - 1), arrival, 0)

    for part in range(parts):
        total = sums_own[part]
        for step in range(1, ncol):
            source = lax.rem(col + step, ncol)
            sum_copy(source, source, part).wait_recv()
            total += sums_in[source, part].astype(jnp.float32)
        normed = layer_norm(total, out_gain[...], out_bias[...]).astype(jnp.bfloat16)
        projected = jnp.dot(normed, w_out[...], preferred_element_type=jnp.float32)
        span = pl.ds(part * sum_rows, sum_rows)
        out_ref[span, :] = (gate[span, :] * projected).astype(jnp.bfloat16)

    def drain_rows(index, carry):
        block, chunk = index // chunks, lax.rem(index, chunks)

        @pl.when(has_up & (block <= row))
        def _():
            up_copy(block, chunk).wait_send()

        @pl.when(has_down & (block >= row))
        def _():
            down_copy(block, chunk).wait_send()

        return carry

    lax.fori_loop(0, nrow * chunks, drain_rows, 0)
    for step in range(1, ncol):
        target = lax.rem(col + step, ncol)
        for part in range(parts):
            sum_copy(target, col, part).wait_send()


def local(nrow, ncol, pair, token_mask, in_gain, in_bias, w_in, w_gate, out_gain, out_bias, w_out):
    row_tok, col_tok, channels = pair.shape
    hidden = w_out.shape[0]
    parts = 3
    row_start = lax.axis_index("row") * row_tok
    col_start = lax.axis_index("col") * col_tok
    row_flags = lax.dynamic_slice_in_dim(token_mask, row_start, row_tok, 0).astype(jnp.float32)
    col_flags = lax.dynamic_slice_in_dim(token_mask, col_start, col_tok, 0).astype(jnp.float32)
    total = row_tok * col_tok
    mask = (row_flags[:, None] * col_flags[None, :]).reshape(total, 1)
    mask_t = (col_flags[:, None] * row_flags[None, :]).reshape(total, 1)
    chunks = row_tok // col_tok * parts
    rows = col_tok // parts * col_tok
    sum_rows = col_tok // parts * row_tok
    padded = -(-row_tok // 8) * 8
    vmem = pl.BlockSpec(memory_space=pltpu.VMEM)
    result = pl.pallas_call(
        functools.partial(kernel, nrow, ncol, row_tok, col_tok, parts),
        out_shape=jax.ShapeDtypeStruct((total, channels), jnp.bfloat16),
        in_specs=[vmem] * 11,
        out_specs=vmem,
        scratch_shapes=[
            pltpu.VMEM((nrow, chunks, rows, hidden), jnp.bfloat16),
            pltpu.VMEM((col_tok, padded, hidden), jnp.float32),
            pltpu.VMEM((total, channels), jnp.float32),
            pltpu.VMEM((rows, hidden), jnp.float32),
            pltpu.VMEM((JTILE * row_tok, hidden), jnp.float32),
            pltpu.VMEM((ncol, parts, sum_rows, hidden), jnp.bfloat16),
            pltpu.VMEM((parts, sum_rows, hidden), jnp.float32),
            pltpu.VMEM((ncol, parts, sum_rows, hidden), jnp.bfloat16),
            pltpu.SemaphoreType.DMA((2, nrow, chunks)),
            pltpu.SemaphoreType.DMA((nrow, chunks)),
            pltpu.SemaphoreType.DMA((ncol, parts)),
            pltpu.SemaphoreType.DMA((ncol, parts)),
        ],
        compiler_params=pltpu.CompilerParams(
            collective_id=0, has_side_effects=True, vmem_limit_bytes=56 * 1024 * 1024
        ),
    )(
        pair.reshape(total, channels),
        pair.transpose(1, 0, 2).reshape(total, channels),
        mask,
        mask_t,
        in_gain[None, :],
        in_bias[None, :],
        w_in,
        w_gate,
        out_gain[None, :],
        out_bias[None, :],
        w_out,
    )
    return result.reshape(col_tok, row_tok, channels).transpose(1, 0, 2)


def solution(mesh):
    placed = (P(("groups", "row"), "col", None), P("groups"), P(), P(), P(), P(), P(), P(), P())
    return jax.shard_map(
        functools.partial(local, mesh.shape["row"], mesh.shape["col"]),
        mesh=mesh,
        in_specs=placed,
        out_specs=P(("groups", "row"), "col", None),
        check_vma=False,
    )
```

```python
import functools

import jax
import jax.numpy as jnp
from jax import lax
from jax.experimental import pallas as pl
from jax.experimental.pallas import tpu as pltpu
from jax.sharding import PartitionSpec as P

MESH = pl.DeviceIdType.MESH
JTILE = 4


def sigmoid(values):
    return 0.5 * jnp.tanh(0.5 * values) + 0.5


def layer_norm(values, gain, bias):
    average = jnp.mean(values, axis=-1, keepdims=True)
    centred = values - average
    variance = jnp.mean(centred * centred, axis=-1, keepdims=True)
    return centred * lax.rsqrt(variance + 1e-05) * gain + bias


def kernel(
    nrow, ncol, row_tok, col_tok, parts,
    pair_ref, flags_ref, in_gain, in_bias, w_in, w_gate, out_gain, out_bias, w_out,
    out_ref,
    blocks, left, gate, flat, turned, wide, stage, sums_out, sums_own, sums_in,
    z_send, z_recv, p_send, p_recv,
):
    hidden = w_out.shape[0]
    group, row, col = lax.axis_index("groups"), lax.axis_index("row"), lax.axis_index("col")
    per_row = row_tok // col_tok
    chunks = per_row * parts
    chunk_j = col_tok // parts
    rows = chunk_j * col_tok
    sum_rows = chunk_j * row_tok
    has_up, has_down = row < nrow - 1, row > 0

    barrier = pltpu.get_barrier_semaphore()

    @pl.when(has_up)
    def _():
        pl.semaphore_signal(barrier, inc=1, device_id=(group, row + 1, col), device_id_type=MESH)

    @pl.when(has_down)
    def _():
        pl.semaphore_signal(barrier, inc=1, device_id=(group, row - 1, col), device_id_type=MESH)

    for step in range(1, ncol):
        peer = lax.rem(col + step, ncol)
        pl.semaphore_signal(barrier, inc=1, device_id=(group, row, peer), device_id_type=MESH)

    def up_copy(block, chunk):
        at = blocks.at[block, chunk]
        return pltpu.make_async_remote_copy(
            at, at, z_send.at[0, block, chunk], z_recv.at[block, chunk], (group, row + 1, col), MESH
        )

    def down_copy(block, chunk):
        at = blocks.at[block, chunk]
        return pltpu.make_async_remote_copy(
            at, at, z_send.at[1, block, chunk], z_recv.at[block, chunk], (group, row - 1, col), MESH
        )

    def sum_copy(target, source, part):
        return pltpu.make_async_remote_copy(
            sums_out.at[target, part], sums_in.at[source, part],
            p_send.at[target, part], p_recv.at[source, part], (group, row, target), MESH,
        )

    gain, bias = in_gain[...], in_bias[...]
    tokens = flags_ref.shape[1]
    flags = flags_ref[...].astype(jnp.float32)

    def pair_mask(outer_start, inner_start, outer, inner):
        place = lax.broadcasted_iota(jnp.int32, (outer * inner, 1), 0).astype(jnp.float32)
        major = jnp.floor((place + 0.5) * (1.0 / inner))
        minor = place - major * inner
        token = lax.broadcasted_iota(jnp.int32, (1, tokens), 1)
        from_major = (token - outer_start).astype(jnp.float32) == major
        from_minor = (token - inner_start).astype(jnp.float32) == minor
        chosen = jnp.where(from_major, flags, 0.0) + jnp.where(from_minor, flags, 0.0)
        count = jnp.dot(
            chosen.astype(jnp.bfloat16), jnp.ones((tokens, hidden), jnp.bfloat16),
            preferred_element_type=jnp.float32,
        )
        return jnp.where(count > 1.5, 1.0, 0.0)

    for chunk in range(chunks):
        span = pl.ds(chunk * rows, rows)
        for j in range(chunk_j):
            at = chunk * chunk_j + j
            flat[at * col_tok : (at + 1) * col_tok, :] = pair_ref[at].astype(jnp.float32)
        normed = layer_norm(flat[span, :], gain, bias).astype(jnp.bfloat16)
        flat[span, :] = normed.astype(jnp.float32)
        proj = jnp.dot(normed, w_in[:, 2 * hidden :], preferred_element_type=jnp.float32)
        right = sigmoid(proj[:, :hidden]) * proj[:, hidden:]
        right *= pair_mask(row * row_tok + chunk * chunk_j, col * col_tok, chunk_j, col_tok)
        blocks[row, chunk] = right.astype(jnp.bfloat16)
        if chunk == 0:
            neighbours = has_up.astype(jnp.int32) + has_down.astype(jnp.int32)
            pl.semaphore_wait(barrier, ncol - 1 + neighbours)

        @pl.when(has_up)
        def _():
            up_copy(row, chunk).start()

        @pl.when(has_down)
        def _():
            down_copy(row, chunk).start()

    k_step = col_tok // parts
    for part in range(parts):
        span = pl.ds(part * sum_rows, sum_rows)
        for k in range(k_step):
            turned[k * row_tok : (k + 1) * row_tok, :] = flat[
                pl.ds(part * k_step + k, row_tok, stride=col_tok), :
            ]
        normed = turned[...].astype(jnp.bfloat16)
        proj = jnp.dot(normed, w_in[:, : 2 * hidden], preferred_element_type=jnp.float32)
        value = sigmoid(proj[:, :hidden]) * proj[:, hidden:]
        value *= pair_mask(col * col_tok + part * k_step, row * row_tok, k_step, row_tok)
        value = value.astype(jnp.bfloat16).astype(jnp.float32)
        for k in range(k_step):
            left[part * k_step + k, :row_tok, :] = value[k * row_tok : (k + 1) * row_tok]
        gate[span, :] = sigmoid(jnp.dot(normed, w_gate[...], preferred_element_type=jnp.float32))

    def partial_sums(block, chunk):
        target, part = block * per_row + chunk // parts, lax.rem(chunk, parts)
        wide[...] = blocks[block, chunk].astype(jnp.float32)

        def tile(at, carry):
            start = pl.multiple_of(at * (JTILE * col_tok), 16)
            totals = [jnp.zeros((row_tok, hidden), jnp.float32) for _ in range(JTILE)]
            for k in range(col_tok):
                lines = left[k, :row_tok, :]
                for j in range(JTILE):
                    totals[j] += wide[pl.ds(start + (j * col_tok + k), 1), :] * lines
            for j in range(JTILE):
                stage[j * row_tok : (j + 1) * row_tok, :] = totals[j]
            span = pl.ds(pl.multiple_of(at * (JTILE * row_tok), 16), JTILE * row_tok)

            @pl.when(target == col)
            def _():
                sums_own[part, span, :] = stage[...]

            @pl.when(target != col)
            def _():
                sums_out[target, part, span, :] = stage[...].astype(jnp.bfloat16)

            return carry

        lax.fori_loop(0, chunk_j // JTILE, tile, 0)

        @pl.when(target != col)
        def _():
            sum_copy(target, col, part).start()

    def own_step(chunk, carry):
        partial_sums(row, chunk)
        return carry

    lax.fori_loop(0, chunks, own_step, 0)

    def arrival(index, carry):
        step = index // (2 * chunks) + 1
        within = lax.rem(index, 2 * chunks)
        chunk, above = within // 2, lax.rem(within, 2)
        block = row - step + above * (2 * step)

        @pl.when((block >= 0) & (block < nrow))
        def _():
            @pl.when(above == 0)
            def _():
                down_copy(block, chunk).wait_recv()

                @pl.when(has_up)
                def _():
                    up_copy(block, chunk).start()

            @pl.when(above == 1)
            def _():
                up_copy(block, chunk).wait_recv()

                @pl.when(has_down)
                def _():
                    down_copy(block, chunk).start()

            partial_sums(block, chunk)

        return carry

    lax.fori_loop(0, 2 * chunks * (nrow - 1), arrival, 0)

    for part in range(parts):
        total = sums_own[part]
        for step in range(1, ncol):
            source = lax.rem(col + step, ncol)
            sum_copy(source, source, part).wait_recv()
            total += sums_in[source, part].astype(jnp.float32)
        normed = layer_norm(total, out_gain[...], out_bias[...]).astype(jnp.bfloat16)
        projected = jnp.dot(normed, w_out[...], preferred_element_type=jnp.float32)
        span = pl.ds(part * sum_rows, sum_rows)
        flat[span, :] = gate[span, :] * projected

    for i in range(row_tok):
        out_ref[i] = flat[pl.ds(i, col_tok, stride=row_tok), :].astype(jnp.bfloat16)

    def drain_rows(index, carry):
        block, chunk = index // chunks, lax.rem(index, chunks)

        @pl.when(has_up & (block <= row))
        def _():
            up_copy(block, chunk).wait_send()

        @pl.when(has_down & (block >= row))
        def _():
            down_copy(block, chunk).wait_send()

        return carry

    lax.fori_loop(0, nrow * chunks, drain_rows, 0)
    for step in range(1, ncol):
        target = lax.rem(col + step, ncol)
        for part in range(parts):
            sum_copy(target, col, part).wait_send()


def local(nrow, ncol, pair, token_mask, in_gain, in_bias, w_in, w_gate, out_gain, out_bias, w_out):
    row_tok, col_tok, channels = pair.shape
    hidden = w_out.shape[0]
    parts = 3
    total = row_tok * col_tok
    chunks = row_tok // col_tok * parts
    rows = col_tok // parts * col_tok
    sum_rows = col_tok // parts * row_tok
    padded = -(-row_tok // 8) * 8
    vmem = pl.BlockSpec(memory_space=pltpu.VMEM)
    result = pl.pallas_call(
        functools.partial(kernel, nrow, ncol, row_tok, col_tok, parts),
        out_shape=jax.ShapeDtypeStruct(pair.shape, jnp.bfloat16),
        in_specs=[vmem] * 9,
        out_specs=vmem,
        scratch_shapes=[
            pltpu.VMEM((nrow, chunks, rows, hidden), jnp.bfloat16),
            pltpu.VMEM((col_tok, padded, hidden), jnp.float32),
            pltpu.VMEM((total, channels), jnp.float32),
            pltpu.VMEM((total, channels), jnp.float32),
            pltpu.VMEM((sum_rows, channels), jnp.float32),
            pltpu.VMEM((rows, hidden), jnp.float32),
            pltpu.VMEM((JTILE * row_tok, hidden), jnp.float32),
            pltpu.VMEM((ncol, parts, sum_rows, hidden), jnp.bfloat16),
            pltpu.VMEM((parts, sum_rows, hidden), jnp.float32),
            pltpu.VMEM((ncol, parts, sum_rows, hidden), jnp.bfloat16),
            pltpu.SemaphoreType.DMA((2, nrow, chunks)),
            pltpu.SemaphoreType.DMA((nrow, chunks)),
            pltpu.SemaphoreType.DMA((ncol, parts)),
            pltpu.SemaphoreType.DMA((ncol, parts)),
        ],
        compiler_params=pltpu.CompilerParams(
            collective_id=0, has_side_effects=True, vmem_limit_bytes=56 * 1024 * 1024
        ),
    )(
        pair,
        token_mask[None, :],
        in_gain[None, :],
        in_bias[None, :],
        w_in,
        w_gate,
        out_gain[None, :],
        out_bias[None, :],
        w_out,
    )
    return result


def solution(mesh):
    placed = (P(("groups", "row"), "col", None), P("groups"), P(), P(), P(), P(), P(), P(), P())
    return jax.shard_map(
        functools.partial(local, mesh.shape["row"], mesh.shape["col"]),
        mesh=mesh,
        in_specs=placed,
        out_specs=P(("groups", "row"), "col", None),
        check_vma=False,
    )
```

```python
import functools

import jax
import jax.numpy as jnp
from jax import lax
from jax.experimental import pallas as pl
from jax.experimental.pallas import tpu as pltpu
from jax.sharding import PartitionSpec as P

MESH = pl.DeviceIdType.MESH
JTILE = 4


def sigmoid(values):
    return 0.5 * jnp.tanh(0.5 * values) + 0.5


def layer_norm(values, gain, bias):
    average = jnp.mean(values, axis=-1, keepdims=True)
    centred = values - average
    variance = jnp.mean(centred * centred, axis=-1, keepdims=True)
    return centred * lax.rsqrt(variance + 1e-05) * gain + bias


def kernel(
    nrow, ncol, row_tok, col_tok, parts,
    *refs,
):
    pair_hbm, hbm_refs, out_ref = refs[0], refs[1:9], refs[9]
    pair_ref, near_refs, pair_sem, near_sem = refs[10], refs[11:19], refs[19], refs[20]
    flags_ref, in_gain, in_bias, w_in, w_gate, out_gain, out_bias, w_out = near_refs
    (
        blocks, left, gate, flat, turned, wide, stage, sums_out, sums_own, sums_in, z_send, z_recv, p_send, p_recv,
    ) = refs[21:]
    hidden = w_out.shape[0]

    def fetch_pair(chunk):
        span = pl.ds(chunk * (col_tok // parts), col_tok // parts)
        return pltpu.make_async_copy(pair_hbm.at[span], pair_ref.at[span], pair_sem.at[chunk])

    def fetch(index):
        return pltpu.make_async_copy(hbm_refs[index], near_refs[index], near_sem.at[index])

    fetch_pair(0).start()
    for index in range(4):
        fetch(index).start()
    for chunk in range(1, row_tok // col_tok * parts):
        fetch_pair(chunk).start()
    for index in range(4, 8):
        fetch(index).start()
    group, row, col = lax.axis_index("groups"), lax.axis_index("row"), lax.axis_index("col")
    per_row = row_tok // col_tok
    chunks = per_row * parts
    chunk_j = col_tok // parts
    rows = chunk_j * col_tok
    sum_rows = chunk_j * row_tok
    has_up, has_down = row < nrow - 1, row > 0

    barrier = pltpu.get_barrier_semaphore()

    @pl.when(has_up)
    def _():
        pl.semaphore_signal(barrier, inc=1, device_id=(group, row + 1, col), device_id_type=MESH)

    @pl.when(has_down)
    def _():
        pl.semaphore_signal(barrier, inc=1, device_id=(group, row - 1, col), device_id_type=MESH)

    for step in range(1, ncol):
        peer = lax.rem(col + step, ncol)
        pl.semaphore_signal(barrier, inc=1, device_id=(group, row, peer), device_id_type=MESH)

    def up_copy(block, chunk):
        at = blocks.at[block, chunk]
        return pltpu.make_async_remote_copy(
            at, at, z_send.at[0, block, chunk], z_recv.at[block, chunk], (group, row + 1, col), MESH
        )

    def down_copy(block, chunk):
        at = blocks.at[block, chunk]
        return pltpu.make_async_remote_copy(
            at, at, z_send.at[1, block, chunk], z_recv.at[block, chunk], (group, row - 1, col), MESH
        )

    def sum_copy(target, source, part):
        return pltpu.make_async_remote_copy(
            sums_out.at[target, part], sums_in.at[source, part],
            p_send.at[target, part], p_recv.at[source, part], (group, row, target), MESH,
        )

    for index in range(4):
        fetch(index).wait()
    gain, bias = in_gain[...], in_bias[...]
    tokens = flags_ref.shape[1]
    flags = flags_ref[...].astype(jnp.float32)

    def pair_mask(outer_start, inner_start, outer, inner):
        place = lax.broadcasted_iota(jnp.int32, (outer * inner, 1), 0).astype(jnp.float32)
        major = jnp.floor((place + 0.5) * (1.0 / inner))
        minor = place - major * inner
        token = lax.broadcasted_iota(jnp.int32, (1, tokens), 1)
        from_major = (token - outer_start).astype(jnp.float32) == major
        from_minor = (token - inner_start).astype(jnp.float32) == minor
        chosen = jnp.where(from_major, flags, 0.0) + jnp.where(from_minor, flags, 0.0)
        count = jnp.dot(
            chosen.astype(jnp.bfloat16), jnp.ones((tokens, hidden), jnp.bfloat16),
            preferred_element_type=jnp.float32,
        )
        return jnp.where(count > 1.5, 1.0, 0.0)

    for chunk in range(chunks):
        span = pl.ds(chunk * rows, rows)
        fetch_pair(chunk).wait()
        for j in range(chunk_j):
            at = chunk * chunk_j + j
            flat[at * col_tok : (at + 1) * col_tok, :] = pair_ref[at].astype(jnp.float32)
        normed = layer_norm(flat[span, :], gain, bias).astype(jnp.bfloat16)
        flat[span, :] = normed.astype(jnp.float32)
        proj = jnp.dot(normed, w_in[:, 2 * hidden :], preferred_element_type=jnp.float32)
        right = sigmoid(proj[:, :hidden]) * proj[:, hidden:]
        right *= pair_mask(row * row_tok + chunk * chunk_j, col * col_tok, chunk_j, col_tok)
        blocks[row, chunk] = right.astype(jnp.bfloat16)
        if chunk == 0:
            neighbours = has_up.astype(jnp.int32) + has_down.astype(jnp.int32)
            pl.semaphore_wait(barrier, ncol - 1 + neighbours)

        @pl.when(has_up)
        def _():
            up_copy(row, chunk).start()

        @pl.when(has_down)
        def _():
            down_copy(row, chunk).start()

    for index in range(4, 8):
        fetch(index).wait()

    k_step = col_tok // parts
    for part in range(parts):
        span = pl.ds(part * sum_rows, sum_rows)
        for k in range(k_step):
            turned[k * row_tok : (k + 1) * row_tok, :] = flat[
                pl.ds(part * k_step + k, row_tok, stride=col_tok), :
            ]
        normed = turned[...].astype(jnp.bfloat16)
        proj = jnp.dot(normed, w_in[:, : 2 * hidden], preferred_element_type=jnp.float32)
        value = sigmoid(proj[:, :hidden]) * proj[:, hidden:]
        value *= pair_mask(col * col_tok + part * k_step, row * row_tok, k_step, row_tok)
        value = value.astype(jnp.bfloat16).astype(jnp.float32)
        for k in range(k_step):
            left[part * k_step + k, :row_tok, :] = value[k * row_tok : (k + 1) * row_tok]
        gate[span, :] = sigmoid(jnp.dot(normed, w_gate[...], preferred_element_type=jnp.float32))

    def partial_sums(block, chunk):
        target, part = block * per_row + chunk // parts, lax.rem(chunk, parts)
        wide[...] = blocks[block, chunk].astype(jnp.float32)

        def tile(at, carry):
            start = pl.multiple_of(at * (JTILE * col_tok), 16)
            totals = [jnp.zeros((row_tok, hidden), jnp.float32) for _ in range(JTILE)]
            for k in range(col_tok):
                lines = left[k, :row_tok, :]
                for j in range(JTILE):
                    totals[j] += wide[pl.ds(start + (j * col_tok + k), 1), :] * lines
            for j in range(JTILE):
                stage[j * row_tok : (j + 1) * row_tok, :] = totals[j]
            span = pl.ds(pl.multiple_of(at * (JTILE * row_tok), 16), JTILE * row_tok)

            @pl.when(target == col)
            def _():
                sums_own[part, span, :] = stage[...]

            @pl.when(target != col)
            def _():
                sums_out[target, part, span, :] = stage[...].astype(jnp.bfloat16)

            return carry

        lax.fori_loop(0, chunk_j // JTILE, tile, 0)

        @pl.when(target != col)
        def _():
            sum_copy(target, col, part).start()

    def own_step(chunk, carry):
        partial_sums(row, chunk)
        return carry

    lax.fori_loop(0, chunks, own_step, 0)

    def arrival(index, carry):
        step = index // (2 * chunks) + 1
        within = lax.rem(index, 2 * chunks)
        chunk, above = within // 2, lax.rem(within, 2)
        block = row - step + above * (2 * step)

        @pl.when((block >= 0) & (block < nrow))
        def _():
            @pl.when(above == 0)
            def _():
                down_copy(block, chunk).wait_recv()

                @pl.when(has_up)
                def _():
                    up_copy(block, chunk).start()

            @pl.when(above == 1)
            def _():
                up_copy(block, chunk).wait_recv()

                @pl.when(has_down)
                def _():
                    down_copy(block, chunk).start()

            partial_sums(block, chunk)

        return carry

    lax.fori_loop(0, 2 * chunks * (nrow - 1), arrival, 0)

    for part in range(parts):
        total = sums_own[part]
        for step in range(1, ncol):
            source = lax.rem(col + step, ncol)
            sum_copy(source, source, part).wait_recv()
            total += sums_in[source, part].astype(jnp.float32)
        normed = layer_norm(total, out_gain[...], out_bias[...]).astype(jnp.bfloat16)
        projected = jnp.dot(normed, w_out[...], preferred_element_type=jnp.float32)
        span = pl.ds(part * sum_rows, sum_rows)
        flat[span, :] = gate[span, :] * projected

    for i in range(row_tok):
        out_ref[i] = flat[pl.ds(i, col_tok, stride=row_tok), :].astype(jnp.bfloat16)

    def drain_rows(index, carry):
        block, chunk = index // chunks, lax.rem(index, chunks)

        @pl.when(has_up & (block <= row))
        def _():
            up_copy(block, chunk).wait_send()

        @pl.when(has_down & (block >= row))
        def _():
            down_copy(block, chunk).wait_send()

        return carry

    lax.fori_loop(0, nrow * chunks, drain_rows, 0)
    for step in range(1, ncol):
        target = lax.rem(col + step, ncol)
        for part in range(parts):
            sum_copy(target, col, part).wait_send()


def local(nrow, ncol, pair, token_mask, in_gain, in_bias, w_in, w_gate, out_gain, out_bias, w_out):
    row_tok, col_tok, channels = pair.shape
    hidden = w_out.shape[0]
    parts = 3
    total = row_tok * col_tok
    chunks = row_tok // col_tok * parts
    rows = col_tok // parts * col_tok
    sum_rows = col_tok // parts * row_tok
    padded = -(-row_tok // 8) * 8
    operands = [pair, token_mask[None, :], in_gain[None, :], in_bias[None, :], w_in, w_gate]
    operands += [out_gain[None, :], out_bias[None, :], w_out]
    scratch = [pltpu.VMEM(operand.shape, operand.dtype) for operand in operands]
    scratch += [
        pltpu.SemaphoreType.DMA((chunks,)),
        pltpu.SemaphoreType.DMA((8,)),
        pltpu.VMEM((nrow, chunks, rows, hidden), jnp.bfloat16),
        pltpu.VMEM((col_tok, padded, hidden), jnp.float32),
        pltpu.VMEM((total, channels), jnp.float32),
        pltpu.VMEM((total, channels), jnp.float32),
        pltpu.VMEM((sum_rows, channels), jnp.float32),
        pltpu.VMEM((rows, hidden), jnp.float32),
        pltpu.VMEM((JTILE * row_tok, hidden), jnp.float32),
        pltpu.VMEM((ncol, parts, sum_rows, hidden), jnp.bfloat16),
        pltpu.VMEM((parts, sum_rows, hidden), jnp.float32),
        pltpu.VMEM((ncol, parts, sum_rows, hidden), jnp.bfloat16),
        pltpu.SemaphoreType.DMA((2, nrow, chunks)),
        pltpu.SemaphoreType.DMA((nrow, chunks)),
        pltpu.SemaphoreType.DMA((ncol, parts)),
        pltpu.SemaphoreType.DMA((ncol, parts)),
    ]
    result = pl.pallas_call(
        functools.partial(kernel, nrow, ncol, row_tok, col_tok, parts),
        out_shape=jax.ShapeDtypeStruct(pair.shape, jnp.bfloat16),
        in_specs=[pl.BlockSpec(memory_space=pltpu.HBM)] * 9,
        out_specs=pl.BlockSpec(memory_space=pltpu.VMEM),
        scratch_shapes=scratch,
        compiler_params=pltpu.CompilerParams(
            collective_id=0, has_side_effects=True, vmem_limit_bytes=56 * 1024 * 1024
        ),
    )(*operands)
    return result


def solution(mesh):
    placed = (P(("groups", "row"), "col", None), P("groups"), P(), P(), P(), P(), P(), P(), P())
    return jax.shard_map(
        functools.partial(local, mesh.shape["row"], mesh.shape["col"]),
        mesh=mesh,
        in_specs=placed,
        out_specs=P(("groups", "row"), "col", None),
        check_vma=False,
    )
```
